128 devices in a mesh: freq: 8 (over x_lo, y), tm: 16 (over z, x_hi, core).
Axes of the slice: x: 4 (x_hi: 2, x_lo: 2; x = x_hi * 2 + x_lo), y: 4, z: 4, core: 2. Of those that a mesh axis runs over, the one named last changes fastest.
Arguments:
- spectra: bfloat16 [2, 64, 2, 256, 3072], P(None, 'tm', None, None, 'freq'), may hold values from -6 to 6
- w_embed: bfloat16 [128, 1024], replicated, may hold values from -0.5 to 0.5
- w_query: bfloat16 [1, 1024, 1024], replicated, may hold values from -1 to 1
- w_key: bfloat16 [1, 1024, 1024], replicated, may hold values from -3 to 3
- w_value: bfloat16 [1, 1024, 1024], replicated, may hold values from -0.1875 to 0.1875
- w_out: bfloat16 [1, 1024, 1024], replicated, may hold values from -0.1875 to 0.1875
- norm_gains: float32 [1, 2, 1024], replicated, may hold values from 0.1 to 1.9
- w_gate: bfloat16 [1, 1024, 2048], replicated, may hold values from -0.1875 to 0.1875
- w_up: bfloat16 [1, 1024, 2048], replicated, may hold values from -0.1875 to 0.1875
- w_down: bfloat16 [1, 2048, 1024], replicated, may hold values from -0.125 to 0.125
- w_head: bfloat16 [1024, 128], replicated, may hold values from -0.1875 to 0.1875
Outputs:
- predicted: bfloat16 [2, 256, 256, 128], P(None, 'tm', 'freq')
The draws below stay inside these ranges and needn't reach their ends.
All inputs are finite; a program needn't handle non-finite values.
Results may differ from the reference program's by a relative error of at most 0.033.
Values may be sent and summed in bfloat16 or wider, within the bound.
A program may use at most 128 MiB of HBM per device.

```python
import math
import jax
import jax.numpy as jnp
from jax import lax

USER_COUNT = 2
ANTENNA_COUNT = 256
SUBCARRIER_COUNT = 3072
SLOT_COUNT = 64
DELAY_TAPS = 256
D = 1024
FF = 2048
HEAD_DIM = 128
TILE = 32
LAYERS = 1
N_FREQ = 8


def own_matrix(key):
    scale = D ** (-0.5)
    return jnp.clip(jax.random.normal(key, (LAYERS, D, D), jnp.float32) * scale, -6.0 * scale, 6.0 * scale)


def draw_w_query(key, part):
    key = jax.random.fold_in(key, 11)
    values = own_matrix(key)
    return values.astype(jnp.bfloat16)


def draw_w_key(key, part):
    key = jax.random.fold_in(key, 12)
    values = own_matrix(key)
    return values.astype(jnp.bfloat16)


def level_of(own_key, dims, split, low, top_value):
    gain = 1.0
    for position, shards_of in split:
        heights = jax.random.uniform(jax.random.fold_in(jax.random.fold_in(own_key, 6), position), (shards_of,), jnp.float32, low / len(split), top_value / len(split))
        gain = gain * jnp.repeat(jnp.exp(heights), dims[position] // shards_of).reshape((-1,) + (1,) * (len(dims) - 1 - position))
    return gain


def scatter_about(rng, extent, scale, most, cuts=(), kind=jnp.bfloat16):
    level = level_of(rng, extent, cuts, -0.22, 0.18) if cuts else 1.0
    drawn = jax.random.normal(rng, extent, jnp.float32) * scale * level
    return jnp.minimum(jnp.maximum(drawn, -most), most).astype(kind)


def setup_inputs(seed: int = 0) -> dict:
    streams_of = jax.random.split(jax.random.key(seed), 12)
    return {
        "spectra": scatter_about(streams_of[0], (USER_COUNT, SLOT_COUNT, 2, ANTENNA_COUNT, SUBCARRIER_COUNT), 1.0, 6.0, ((1, 16), (4, 8))),
        "w_embed": scatter_about(streams_of[1], (2 * SLOT_COUNT, D), (2 * SLOT_COUNT) ** -0.5, 0.5),
        "w_query": draw_w_query(jax.random.fold_in(streams_of[11], 71), 0),
        "w_key": draw_w_key(jax.random.fold_in(streams_of[11], 71), 0),
        "w_value": scatter_about(streams_of[4], (LAYERS, D, D), D ** -0.5, 0.1875),
        "w_out": scatter_about(streams_of[5], (LAYERS, D, D), D ** -0.5, 0.1875),
        "norm_gains": jnp.clip(1.0 + 0.18 * jax.random.normal(streams_of[6], (LAYERS, 2, D), jnp.float32), 0.1, 1.9),
        "w_gate": scatter_about(streams_of[7], (LAYERS, D, FF), D ** -0.5, 0.1875),
        "w_up": scatter_about(streams_of[8], (LAYERS, D, FF), D ** -0.5, 0.1875),
        "w_down": scatter_about(streams_of[9], (LAYERS, FF, D), FF ** -0.5, 0.125),
        "w_head": scatter_about(streams_of[10], (D, 2 * SLOT_COUNT), D ** -0.5, 0.1875),
    }


def fourier_table(first, count, out_first, out_count, total):
    rows = first + jnp.arange(count, dtype=jnp.int32)
    cols = out_first + jnp.arange(out_count, dtype=jnp.int32)
    product = rows[:, None] * cols[None, :] % total
    angle = 2.0 * math.pi / total * product.astype(jnp.float32)
    factor = 1.0 / math.sqrt(total)
    cosine = jnp.cos(angle) * factor
    sine = jnp.sin(angle) * factor
    real_rows = jnp.stack([cosine, -sine], axis=-1)
    imag_rows = jnp.stack([sine, cosine], axis=-1)
    return jnp.stack([real_rows, imag_rows], axis=0).astype(jnp.bfloat16)

def normed(values):
    return values * lax.rsqrt(lax.optimization_barrier(jnp.mean(values * values, axis=-1, keepdims=True)) + 1e-05)

def network(feature_rows, w_embed, w_query, w_key, w_value, w_out, norm_gains, w_gate, w_up, w_down, w_head):
    count = feature_rows.shape[0]
    width = w_embed.shape[1]
    heads = width // HEAD_DIM
    state = jnp.dot(feature_rows, w_embed, preferred_element_type=jnp.float32).astype(jnp.bfloat16)
    for layer in range(w_query.shape[0]):
        hnorm = (normed(state.astype(jnp.float32)) * norm_gains[layer, 0]).astype(jnp.bfloat16)
        query = jnp.dot(hnorm, w_query[layer], preferred_element_type=jnp.float32).astype(jnp.bfloat16)
        keyed = jnp.dot(hnorm, w_key[layer], preferred_element_type=jnp.float32).astype(jnp.bfloat16)
        valued = jnp.dot(hnorm, w_value[layer], preferred_element_type=jnp.float32).astype(jnp.bfloat16)
        shape4 = (count // TILE, TILE, heads, HEAD_DIM)
        scores = jnp.einsum('bqhd,bkhd->bhqk', query.reshape(shape4).astype(jnp.float32), keyed.reshape(shape4).astype(jnp.float32)) * HEAD_DIM ** (-0.5)
        weights = jax.nn.softmax(scores, axis=-1).astype(jnp.bfloat16)
        mixed = jnp.einsum('bhqk,bkhd->bqhd', weights.astype(jnp.float32), valued.reshape(shape4).astype(jnp.float32)).astype(jnp.bfloat16).reshape(count, width)
        state = (state.astype(jnp.float32) + jnp.dot(mixed, w_out[layer], preferred_element_type=jnp.float32)).astype(jnp.bfloat16)
        hnorm = (normed(state.astype(jnp.float32)) * norm_gains[layer, 1]).astype(jnp.bfloat16)
        gate = jnp.dot(hnorm, w_gate[layer], preferred_element_type=jnp.float32)
        upward = jnp.dot(hnorm, w_up[layer], preferred_element_type=jnp.float32)
        hidden = (jax.nn.silu(gate) * upward).astype(jnp.bfloat16)
        state = (state.astype(jnp.float32) + jnp.dot(hidden, w_down[layer], preferred_element_type=jnp.float32)).astype(jnp.bfloat16)
    final = normed(state.astype(jnp.float32)).astype(jnp.bfloat16)
    return jnp.dot(final, w_head, preferred_element_type=jnp.float32).astype(jnp.bfloat16)

def reference(spectra, w_embed, w_query, w_key, w_value, w_out, norm_gains, w_gate, w_up, w_down, w_head):
    block_length = SUBCARRIER_COUNT // N_FREQ
    delay_table = fourier_table(0, SUBCARRIER_COUNT, 0, DELAY_TAPS, SUBCARRIER_COUNT).astype(jnp.float32).reshape(2, N_FREQ, block_length, DELAY_TAPS, 2)
    doppler_table = fourier_table(0, SLOT_COUNT, 0, SLOT_COUNT, SLOT_COUNT).astype(jnp.float32)

    def per_slot(block_piece):
        split_parts = block_piece.astype(jnp.float32).reshape(USER_COUNT, 2, ANTENNA_COUNT, N_FREQ, block_length)
        partial_sums = jnp.einsum('ucagf,cgfte->gueat', split_parts, delay_table).astype(jnp.bfloat16)
        partial_sums = lax.optimization_barrier(partial_sums)
        return lax.optimization_barrier(jnp.sum(partial_sums.astype(jnp.float32), axis=0)).astype(jnp.bfloat16)
    tap_values = lax.map(per_slot, jnp.moveaxis(spectra, 1, 0))
    feature_rows = jnp.einsum('sucat,cske->uatek', tap_values.astype(jnp.float32), doppler_table).astype(jnp.bfloat16)
    token_rows = feature_rows.reshape(USER_COUNT * ANTENNA_COUNT // 8, 8 * DELAY_TAPS, 2 * SLOT_COUNT)

    def per_group(group):
        return network(group, w_embed, w_query, w_key, w_value, w_out, norm_gains, w_gate, w_up, w_down, w_head)
    result_values = lax.map(per_group, token_rows)
    return result_values.reshape(USER_COUNT, ANTENNA_COUNT, DELAY_TAPS, 2 * SLOT_COUNT)
```

```python
import math

import jax
import jax.numpy as jnp
import ml_dtypes
import numpy as np
from jax import lax
from jax.experimental import pallas as pl
from jax.experimental.pallas import tpu as pltpu
from jax.sharding import PartitionSpec as P

BF = jnp.bfloat16
F32 = jnp.float32
MESH = pl.DeviceIdType.MESH

SUBCARRIERS = 3072
TAPS = 256
SLOTS = 64
TILE = 32
FREQ = 8
XN, YN = 2, 4
TM = 16
D = 1024
FF = 2048
CHUNKS = 4
ROWS = 256
BLOCK = 128
OFFSETS = [(dx, dy) for dx in (1, 0) for dy in (2, 1, 3, 0) if (dx, dy) != (0, 0)]


def dot(a, b):
    return jnp.dot(a, b, preferred_element_type=F32)


def delay_tables():
    share = SUBCARRIERS // FREQ
    f = np.arange(SUBCARRIERS)[:, None]
    t = np.arange(TAPS)[None, :]
    angle = 2.0 * math.pi / SUBCARRIERS * (f * t % SUBCARRIERS)
    r = 1.0 / math.sqrt(SUBCARRIERS)
    cosine, sine = np.cos(angle) * r, np.sin(angle) * r
    table = np.stack([np.stack([cosine, -sine], 1), np.stack([sine, cosine], 1)], 0)
    table = table.reshape(2, FREQ, share, 2, XN, YN, TILE)
    table = table.transpose(1, 0, 2, 5, 4, 3, 6)
    both = np.stack([table, table[:, :, :, :, ::-1]], 0)
    return both.reshape(2, FREQ, 2 * share, 2 * TAPS).astype(ml_dtypes.bfloat16)


def doppler_tables():
    s = np.arange(SLOTS)[:, None]
    k = np.arange(SLOTS)[None, :]
    angle = 2.0 * math.pi / SLOTS * (s * k % SLOTS)
    r = 1.0 / math.sqrt(SLOTS)
    cosine, sine = np.cos(angle) * r, np.sin(angle) * r
    table = np.stack([np.stack([cosine, -sine], 1), np.stack([sine, cosine], 1)], 0)
    table = table.reshape(2, TM, 2, 2, 2 * SLOTS)
    table = table.transpose(3, 0, 1, 2, 4)
    out = np.zeros((XN, 2, 2, 4, TM, 2, 4, 2 * SLOTS))
    for a in range(4):
        out[0, :, :, a, :, :, a] = table
        out[1, :, :, a, :, :, a] = table[::-1]
    return out.reshape(XN, 512, 512).astype(ml_dtypes.bfloat16)


def normed(x):
    return x * lax.rsqrt(jnp.mean(x * x, axis=-1, keepdims=True) + 1e-05)


def kernel(
    spectra, tables, doppler, w_embed, w_query, w_key, w_value, w_out, gains, w_gate, w_up, w_down, w_head,
    out,
    spec, tab_a, tab_b, dop, ve, vq, vk, vv, vo, vg, vu, vd, vh,
    part, got, taps, tiles, wide, feats, xs, hs, ms, hid,
    load_sem, part_send, part_recv, tile_send, tile_recv,
):
    freq = lax.axis_index("freq")
    tm = lax.axis_index("tm")
    mx, my = freq // YN, freq % YN

    loads = [
        (tables.at[0, freq], tab_a),
        (tables.at[1, freq], tab_b),
        (spectra.at[0], spec.at[0]),
        (spectra.at[1], spec.at[1]),
        (doppler.at[mx], dop),
        (w_embed, ve),
        (w_query.at[0], vq),
        (w_key.at[0], vk),
        (w_value.at[0], vv),
        (w_out.at[0], vo),
        (w_gate.at[0], vg),
        (w_up.at[0], vu),
        (w_down.at[0], vd),
        (w_head, vh),
    ]
    loads = [pltpu.make_async_copy(a, b, load_sem.at[i]) for i, (a, b) in enumerate(loads)]
    for load in loads:
        load.start()

    def peer(dx, dy):
        return (mx + dx) % XN * YN + (my + dy) % YN

    barrier = pltpu.get_barrier_semaphore()
    for dx, dy in OFFSETS:
        pl.semaphore_signal(barrier, inc=1, device_id={"freq": peer(dx, dy)}, device_id_type=MESH)

    def greet(i, _):
        pl.semaphore_signal(barrier, inc=1, device_id={"tm": (tm + i) % TM}, device_id_type=MESH)
        return 0

    lax.fori_loop(1, TM, greet, 0)

    low = lax.broadcasted_iota(jnp.int32, (ROWS, 128), 1) < 64

    def transform(u):
        for yp in range(2):
            cols = slice(256 * yp, 256 * yp + 256)
            sums = []
            for s in range(4):
                x = jnp.concatenate([spec[u, s, 0], spec[u, s, 1]], axis=1)
                sums.append(dot(x, (tab_b if s % 2 else tab_a)[:, cols]))
            for yy in range(2):
                a = [v[:, 128 * yy : 128 * yy + 128] for v in sums]
                for x in range(XN):
                    pair = [jnp.where(low, a[2 * sp + x], a[2 * sp + 1 - x]) for sp in range(2)]
                    pair = [v.reshape(TM, 2, 8, 128) for v in pair]
                    for ah in range(2):
                        rows = jnp.stack([pair[0][:, ah], pair[1][:, ah]], axis=1).reshape(ROWS, 128)
                        part[2 * u + ah, x * YN + 2 * yp + yy] = rows.astype(BF)

    def part_copy(c, i):
        dx, dy = OFFSETS[i]
        target = peer(dx, dy)
        return pltpu.make_async_remote_copy(
            src_ref=part.at[c, target],
            dst_ref=got.at[c, i],
            send_sem=part_send.at[c],
            recv_sem=part_recv.at[c],
            device_id={"freq": target},
            device_id_type=MESH,
        )

    def part_all(c):
        return pltpu.make_async_remote_copy(
            src_ref=part.at[c, pl.ds(0, FREQ - 1)],
            dst_ref=got.at[c],
            send_sem=part_send.at[c],
            recv_sem=part_recv.at[c],
            device_id={"freq": peer(0, 1)},
            device_id_type=MESH,
        )

    def tile_copy(c, i):
        target = (tm + i) % TM
        return pltpu.make_async_remote_copy(
            src_ref=taps.at[c, target],
            dst_ref=tiles.at[c, tm],
            send_sem=tile_send.at[c],
            recv_sem=tile_recv.at[c],
            device_id={"tm": target},
            device_id_type=MESH,
        )

    def tile_all(c):
        return pltpu.make_async_remote_copy(
            src_ref=taps.at[c, pl.ds(0, TM - 1)],
            dst_ref=tiles.at[c, pl.ds(0, TM - 1)],
            send_sem=tile_send.at[c],
            recv_sem=tile_recv.at[c],
            device_id={"tm": (tm + 1) % TM},
            device_id_type=MESH,
        )

    for i in range(3):
        loads[i].wait()
    transform(0)
    pl.semaphore_wait(barrier, FREQ - 1 + TM - 1)
    for c in (0, 1):
        for i in range(FREQ - 1):
            part_copy(c, i).start()
    loads[3].wait()
    transform(1)
    for c in (2, 3):
        for i in range(FREQ - 1):
            part_copy(c, i).start()

    def reduce(c):
        part_all(c).wait_recv()
        total = part[c, freq].astype(F32)
        for i in range(FREQ - 1):
            total = total + got[c, i].astype(F32)
        taps[c] = total.astype(BF).reshape(TM, 16, 128)

        def send(i, _):
            tile_copy(c, i).start()
            return 0

        lax.fori_loop(1, TM, send, 0)
        tiles[c, tm] = taps[c, tm]

    reduce(0)
    for load in loads[4:]:
        load.wait()

    same_tile = (
        lax.broadcasted_iota(jnp.int32, (BLOCK, BLOCK), 0) // TILE
        == lax.broadcasted_iota(jnp.int32, (BLOCK, BLOCK), 1) // TILE
    )
    spans = [(j, b) for j in range(2) for b in range(ROWS // BLOCK)]

    def doppler_of(c):
        tile_all(c).wait_recv()
        wide[...] = tiles[c].astype(F32).reshape(ROWS, 128)
        groups = []
        for g in range(2):
            stacked = jnp.concatenate([wide[pl.ds(4 * g + a, 32, stride=8), :] for a in range(4)], axis=0)
            turned = stacked.T.astype(BF)
            groups.append(jnp.concatenate([turned[32 * q : 32 * q + 32] for q in range(4)], axis=1))
        spread = dot(jnp.concatenate(groups, axis=0), dop[...]).astype(BF)
        for g in range(2):
            for a in range(4):
                first = 32 * (4 * g + a)
                feats[first : first + 32, :] = spread[32 * g : 32 * g + 32, 128 * a : 128 * a + 128]

    def norm_rows(gain):
        for r in range(0, ROWS, 64):
            rows = slice(r, r + 64)
            value = normed(xs[rows, :].astype(F32))
            hs[rows, :] = (value if gain is None else value * gains[0, gain : gain + 1, :]).astype(BF)

    def attend(hp, scores, v):
        scores = [jnp.where(same_tile, s, -1e30) for s in scores]
        tops = [jnp.max(s, axis=-1, keepdims=True) for s in scores]
        weights = [jnp.exp((s - m) * 128**-0.5) for s, m in zip(scores, tops)]
        sums = [jnp.sum(p, axis=-1, keepdims=True) for p in weights]
        weights = [(p * (1.0 / t)).astype(BF) for p, t in zip(weights, sums)]
        for p, (j, b) in zip(weights, spans):
            rows = slice(b * BLOCK, (b + 1) * BLOCK)
            first = hp * 256 + j * 128
            ms[rows, first : first + 128] = dot(p, v[rows, j * 128 : (j + 1) * 128]).astype(BF)

    def chunk(c, _):
        doppler_of(c)
        for n in range(0, D, 256):
            cols = slice(n, n + 256)
            xs[:, cols] = dot(feats[...], ve[:, cols]).astype(BF)
        norm_rows(0)
        waiting = []
        for hp in range(4):
            cols = slice(hp * 256, hp * 256 + 256)
            q = dot(hs[...], vq[:, cols]).astype(BF)
            k = dot(hs[...], vk[:, cols]).astype(BF)
            v = dot(hs[...], vv[:, cols]).astype(BF)
            scores = []
            for j, b in spans:
                rows, part_cols = slice(b * BLOCK, (b + 1) * BLOCK), slice(j * 128, (j + 1) * 128)
                scores.append(
                    lax.dot_general(
                        q[rows, part_cols], k[rows, part_cols], (((1,), (1,)), ((), ())), preferred_element_type=F32
                    )
                )
            waiting.append((hp, scores, v))
            if hp:
                attend(*waiting.pop(0))
        attend(*waiting.pop(0))
        for n in range(0, D, 256):
            cols = slice(n, n + 256)
            xs[:, cols] = (xs[:, cols].astype(F32) + dot(ms[...], vo[:, cols])).astype(BF)

        @pl.when(c < CHUNKS - 1)
        def _():
            reduce(c + 1)

        norm_rows(1)
        for n in range(0, FF, 256):
            cols = slice(n, n + 256)
            gate = dot(hs[...], vg[:, cols])
            up = dot(hs[...], vu[:, cols])
            hid[:, cols] = (jax.nn.silu(gate) * up).astype(BF)
        for n in range(0, D, 256):
            cols = slice(n, n + 256)
            xs[:, cols] = (xs[:, cols].astype(F32) + dot(hid[...], vd[:, cols])).astype(BF)
        norm_rows(None)
        out[c] = dot(hs[...], vh[...]).astype(BF)
        return 0

    lax.fori_loop(0, CHUNKS, chunk, 0)

    def drain(c, _):
        part_all(c).wait_send()
        tile_all(c).wait_send()
        return 0

    lax.fori_loop(0, CHUNKS, drain, 0)


def body(spectra, w_embed, w_query, w_key, w_value, w_out, norm_gains, w_gate, w_up, w_down, w_head):
    vmem, dma = pltpu.VMEM, pltpu.SemaphoreType.DMA
    hbm = pl.BlockSpec(memory_space=pl.ANY)
    near = pl.BlockSpec(memory_space=pltpu.VMEM)
    result = pl.pallas_call(
        kernel,
        out_shape=jax.ShapeDtypeStruct((CHUNKS, ROWS, 2 * SLOTS), BF),
        in_specs=[hbm] * 8 + [near] + [hbm] * 4,
        out_specs=near,
        scratch_shapes=[
            vmem((2, 4, 2, 256, 384), BF),
            vmem((768, 512), BF),
            vmem((768, 512), BF),
            vmem((512, 512), BF),
            vmem((2 * SLOTS, D), BF),
            vmem((D, D), BF),
            vmem((D, D), BF),
            vmem((D, D), BF),
            vmem((D, D), BF),
            vmem((D, FF), BF),
            vmem((D, FF), BF),
            vmem((FF, D), BF),
            vmem((D, 2 * SLOTS), BF),
            vmem((CHUNKS, FREQ, ROWS, 128), BF),
            vmem((CHUNKS, FREQ - 1, ROWS, 128), BF),
            vmem((CHUNKS, TM, 16, 128), BF),
            vmem((CHUNKS, TM, 16, 128), BF),
            vmem((ROWS, 128), F32),
            vmem((ROWS, 128), BF),
            vmem((ROWS, D), BF),
            vmem((ROWS, D), BF),
            vmem((ROWS, D), BF),
            vmem((ROWS, FF), BF),
            dma((14,)),
            dma((CHUNKS,)),
            dma((CHUNKS,)),
            dma((CHUNKS,)),
            dma((CHUNKS,)),
        ],
        compiler_params=pltpu.CompilerParams(collective_id=0, has_side_effects=True, vmem_limit_bytes=58 << 20),
        name="fused",
    )(
        spectra, jnp.asarray(delay_tables()), jnp.asarray(doppler_tables()),
        w_embed, w_query, w_key, w_value, w_out, norm_gains, w_gate, w_up, w_down, w_head,
    )
    return result.reshape(2, 16, TILE, 2 * SLOTS)


def solution(mesh):
    placed = (P(None, "tm", None, None, "freq"), P(), P(), P(), P(), P(), P(), P(), P(), P(), P())
    return jax.shard_map(
        body, mesh=mesh, in_specs=placed, out_specs=P(None, "tm", "freq", None), check_vma=False
    )
```

```python
import math

import jax
import jax.numpy as jnp
import ml_dtypes
import numpy as np
from jax import lax
from jax.experimental import pallas as pl
from jax.experimental.pallas import tpu as pltpu
from jax.sharding import PartitionSpec as P

BF = jnp.bfloat16
F32 = jnp.float32
MESH = pl.DeviceIdType.MESH

SUBCARRIERS = 3072
TAPS = 256
SLOTS = 64
TILE = 32
FREQ = 8
XN, YN = 2, 4
TM = 16
D = 1024
FF = 2048
CHUNKS = 4
ROWS = 256
BLOCK = 128
HALF = ROWS // 2


def dot(a, b):
    return jnp.dot(a, b, preferred_element_type=F32)


def delay_tables():
    share = SUBCARRIERS // FREQ
    f = np.arange(SUBCARRIERS)[:, None]
    t = np.arange(TAPS)[None, :]
    angle = 2.0 * math.pi / SUBCARRIERS * (f * t % SUBCARRIERS)
    r = 1.0 / math.sqrt(SUBCARRIERS)
    cosine, sine = np.cos(angle) * r, np.sin(angle) * r
    table = np.stack([np.stack([cosine, -sine], 1), np.stack([sine, cosine], 1)], 0)
    table = table.reshape(2, FREQ, share, 2, XN, YN, TILE)
    table = table.transpose(1, 0, 2, 5, 4, 3, 6)
    both = np.stack([table, table[:, :, :, :, ::-1]], 0)
    return both.reshape(2, FREQ, 2 * share, 2 * TAPS).astype(ml_dtypes.bfloat16)


def doppler_tables():
    s = np.arange(SLOTS)[:, None]
    k = np.arange(SLOTS)[None, :]
    angle = 2.0 * math.pi / SLOTS * (s * k % SLOTS)
    r = 1.0 / math.sqrt(SLOTS)
    cosine, sine = np.cos(angle) * r, np.sin(angle) * r
    table = np.stack([np.stack([cosine, -sine], 1), np.stack([sine, cosine], 1)], 0)
    table = table.reshape(2, TM, 2, 2, 2 * SLOTS)
    table = table.transpose(3, 0, 1, 2, 4)
    out = np.zeros((XN, 2, 2, 4, TM, 2, 4, 2 * SLOTS))
    for a in range(4):
        out[0, :, :, a, :, :, a] = table
        out[1, :, :, a, :, :, a] = table[::-1]
    return out.reshape(XN, 512, 512).astype(ml_dtypes.bfloat16)


def normed(x):
    return x * lax.rsqrt(jnp.mean(x * x, axis=-1, keepdims=True) + 1e-05)


def kernel(
    spectra, tables, doppler, w_embed, w_query, w_key, w_value, w_out, gains, w_gate, w_up, w_down, w_head,
    out,
    spec, tab_a, tab_b, dop, ve, vq, vk, vv, vo, vg, vu, vd, vh,
    part_a, part_b, got_a, got_b, sum_a, sum_b, last_a, last_b, taps, tiles, wide, feats, xs, hs, ms, hid,
    load_sem, sends, recvs, meet,
):
    freq = lax.axis_index("freq")
    tm = lax.axis_index("tm")
    mx, my = lax.div(freq, YN), lax.rem(freq, YN)

    loads = [
        (tables.at[0, freq], tab_a),
        (tables.at[1, freq], tab_b),
        (spectra.at[0], spec.at[0]),
        (spectra.at[1], spec.at[1]),
        (doppler.at[mx], dop),
        (w_embed, ve),
        (w_query.at[0], vq),
        (w_key.at[0], vk),
        (w_value.at[0], vv),
        (w_out.at[0], vo),
        (w_gate.at[0], vg),
        (w_up.at[0], vu),
        (w_down.at[0], vd),
        (w_head, vh),
    ]
    loads = [pltpu.make_async_copy(a, b, load_sem.at[i]) for i, (a, b) in enumerate(loads)]
    for load in loads[:3]:
        load.start()

    other_x = (1 - mx) * YN + my

    def along_y(i):
        return lax.rem(my + 1 + i, YN)

    tz, th, tc = lax.div(tm, 4), lax.rem(lax.div(tm, 2), 2), lax.rem(tm, 2)
    other_h = tz * 4 + (1 - th) * 2 + tc
    other_c = tz * 4 + th * 2 + (1 - tc)
    barrier = pltpu.get_barrier_semaphore()
    for i in range(YN - 1):
        pl.semaphore_signal(barrier, inc=1, device_id={"freq": mx * YN + along_y(i)}, device_id_type=MESH)
    pl.semaphore_signal(barrier, inc=1, device_id={"freq": other_x}, device_id_type=MESH)
    for i in range(1, 4):
        pl.semaphore_signal(barrier, inc=1, device_id={"tm": lax.rem(tm + 4 * i, TM)}, device_id_type=MESH)
    for other in (other_h, other_c):
        pl.semaphore_signal(barrier, inc=1, device_id={"tm": other}, device_id_type=MESH)

    low = lax.broadcasted_iota(jnp.int32, (ROWS, 128), 1) < 64

    def transform(u):
        for yp in range(2):
            cols = slice(256 * yp, 256 * yp + 256)
            sums = []
            for s in range(4):
                x = jnp.concatenate([spec[u, s, 0], spec[u, s, 1]], axis=1)
                sums.append(dot(x, (tab_b if s % 2 else tab_a)[:, cols]))
            for yy in range(2):
                a = [v[:, 128 * yy : 128 * yy + 128] for v in sums]
                for x in range(XN):
                    pair = [jnp.where(low, a[2 * sp + x], a[2 * sp + 1 - x]) for sp in range(2)]
                    pair = [v.reshape(TM, 2, 8, 128) for v in pair]
                    for ah in range(2):
                        rows = jnp.stack([pair[0][:, ah], pair[1][:, ah]], axis=1).reshape(ROWS, 128)
                        part_a[2 * u + ah, 2 * yp + yy, x] = rows[:HALF].astype(BF)
                        part_b[2 * u + ah, x, 2 * yp + yy] = rows[HALF:].astype(BF)

    def remote(src, dst, kind, c, device):
        return pltpu.make_async_remote_copy(
            src_ref=src,
            dst_ref=dst,
            send_sem=sends.at[kind, c],
            recv_sem=recvs.at[kind, c],
            device_id=device,
            device_id_type=MESH,
        )

    near_x = {"freq": other_x}

    def copy_a(c, i):
        y = along_y(i)
        return remote(part_a.at[c, y], got_a.at[c, i], 0, c, {"freq": mx * YN + y})

    def copy_b(c):
        return remote(part_b.at[c, 1 - mx], got_b.at[c], 1, c, near_x)

    def copy_sum_a(c):
        return remote(sum_a.at[c, 1 - mx], last_a.at[c], 2, c, near_x)

    def copy_sum_b(c, i):
        y = along_y(i)
        return remote(sum_b.at[c, y], last_b.at[c, i], 3, c, {"freq": mx * YN + y})

    def all_a(c):
        return remote(part_a.at[c, pl.ds(0, YN - 1)], got_a.at[c], 0, c, near_x)

    def all_sum_b(c):
        return remote(sum_b.at[c, pl.ds(0, YN - 1)], last_b.at[c], 3, c, near_x)

    def start_parts(c):
        copy_b(c).start()
        for i in (1, 0, 2):
            copy_a(c, i).start()

    def middle(c):
        all_a(c).wait_recv()
        for x in range(XN):
            total = part_a[c, my, x].astype(F32)
            for i in range(YN - 1):
                total = total + got_a[c, i, x].astype(F32)
            sum_a[c, x] = total.astype(BF)
        copy_sum_a(c).start()
        copy_b(c).wait_recv()
        for y in range(YN):
            sum_b[c, y] = (part_b[c, mx, y].astype(F32) + got_b[c, y].astype(F32)).astype(BF)
        for i in (1, 0, 2):
            copy_sum_b(c, i).start()

    def copy_tile(c, i):
        target = lax.rem(tm + i, TM)
        return remote(taps.at[c, target], tiles.at[c, tm], 4, c, {"tm": target})

    def all_tiles(c):
        return remote(taps.at[c, pl.ds(0, TM - 1)], tiles.at[c, pl.ds(0, TM - 1)], 4, c, {"tm": other_c})

    for load in loads[:3]:
        load.wait()
    for load in loads[3:]:
        load.start()
    transform(0)
    pl.semaphore_wait(barrier, 9)
    start_parts(0)
    pl.semaphore_signal(meet.at[0], inc=1, device_id={"tm": other_h}, device_id_type=MESH)
    loads[3].wait()
    transform(1)
    pl.semaphore_wait(meet.at[0], 1)
    pl.semaphore_signal(meet.at[1], inc=1, device_id={"tm": other_c}, device_id_type=MESH)
    pl.semaphore_wait(meet.at[1], 1)

    def reduce(c):
        copy_sum_a(c).wait_recv()
        taps[c, 0:8] = (sum_a[c, mx].astype(F32) + last_a[c].astype(F32)).astype(BF).reshape(TM // 2, 16, 128)
        all_sum_b(c).wait_recv()
        total = sum_b[c, my].astype(F32)
        for i in range(YN - 1):
            total = total + last_b[c, i].astype(F32)
        taps[c, 8:16] = total.astype(BF).reshape(TM // 2, 16, 128)

        def send(i, _):
            copy_tile(c, i).start()
            return 0

        lax.fori_loop(1, TM, send, 0)
        tiles[c, tm] = taps[c, tm]

    middle(0)
    start_parts(1)
    reduce(0)
    middle(1)
    start_parts(2)
    start_parts(3)
    for load in loads[4:]:
        load.wait()

    same_tile = (
        lax.broadcasted_iota(jnp.int32, (BLOCK, BLOCK), 0) // TILE
        == lax.broadcasted_iota(jnp.int32, (BLOCK, BLOCK), 1) // TILE
    )
    spans = [(j, b) for j in range(2) for b in range(ROWS // BLOCK)]

    def doppler_of(c):
        all_tiles(c).wait_recv()
        wide[...] = tiles[c].astype(F32).reshape(ROWS, 128)
        groups = []
        for g in range(2):
            stacked = jnp.concatenate([wide[pl.ds(4 * g + a, 32, stride=8), :] for a in range(4)], axis=0)
            turned = stacked.T.astype(BF)
            groups.append(jnp.concatenate([turned[32 * q : 32 * q + 32] for q in range(4)], axis=1))
        spread = dot(jnp.concatenate(groups, axis=0), dop[...]).astype(BF)
        for g in range(2):
            for a in range(4):
                first = 32 * (4 * g + a)
                feats[first : first + 32, :] = spread[32 * g : 32 * g + 32, 128 * a : 128 * a + 128]

    def norm_rows(gain):
        for r in range(0, ROWS, 64):
            rows = slice(r, r + 64)
            value = normed(xs[rows, :].astype(F32))
            hs[rows, :] = (value if gain is None else value * gains[0, gain : gain + 1, :]).astype(BF)

    def attend(hp, scores, v):
        scores = [jnp.where(same_tile, s, -1e30) for s in scores]
        tops = [jnp.max(s, axis=-1, keepdims=True) for s in scores]
        weights = [jnp.exp((s - m) * 128**-0.5) for s, m in zip(scores, tops)]
        sums = [jnp.sum(p, axis=-1, keepdims=True) for p in weights]
        weights = [(p * (1.0 / t)).astype(BF) for p, t in zip(weights, sums)]
        for p, (j, b) in zip(weights, spans):
            rows = slice(b * BLOCK, (b + 1) * BLOCK)
            first = hp * 256 + j * 128
            ms[rows, first : first + 128] = dot(p, v[rows, j * 128 : (j + 1) * 128]).astype(BF)

    def chunk(c, _):
        doppler_of(c)
        pl.when(c < CHUNKS - 1)(lambda: reduce(c + 1))
        for n in range(0, D, 256):
            cols = slice(n, n + 256)
            xs[:, cols] = dot(feats[...], ve[:, cols]).astype(BF)
        norm_rows(0)
        waiting = []
        for hp in range(4):
            cols = slice(hp * 256, hp * 256 + 256)
            q = dot(hs[...], vq[:, cols]).astype(BF)
            k = dot(hs[...], vk[:, cols]).astype(BF)
            v = dot(hs[...], vv[:, cols]).astype(BF)
            scores = []
            for j, b in spans:
                rows, part_cols = slice(b * BLOCK, (b + 1) * BLOCK), slice(j * 128, (j + 1) * 128)
                scores.append(
                    lax.dot_general(
                        q[rows, part_cols], k[rows, part_cols], (((1,), (1,)), ((), ())), preferred_element_type=F32
                    )
                )
            waiting.append((hp, scores, v))
            if hp:
                attend(*waiting.pop(0))
        attend(*waiting.pop(0))
        for n in range(0, D, 256):
            cols = slice(n, n + 256)
            xs[:, cols] = (xs[:, cols].astype(F32) + dot(ms[...], vo[:, cols])).astype(BF)

        pl.when(c < CHUNKS - 2)(lambda: middle(c + 2))

        norm_rows(1)
        for n in range(0, FF, 256):
            cols = slice(n, n + 256)
            gate = dot(hs[...], vg[:, cols])
            up = dot(hs[...], vu[:, cols])
            hid[:, cols] = (jax.nn.silu(gate) * up).astype(BF)
        for n in range(0, D, 256):
            cols = slice(n, n + 256)
            xs[:, cols] = (xs[:, cols].astype(F32) + dot(hid[...], vd[:, cols])).astype(BF)
        norm_rows(None)
        out[c] = dot(hs[...], vh[...]).astype(BF)
        return 0

    lax.fori_loop(0, CHUNKS, chunk, 0)

    def drain(c, _):
        all_a(c).wait_send()
        copy_b(c).wait_send()
        copy_sum_a(c).wait_send()
        all_sum_b(c).wait_send()
        all_tiles(c).wait_send()
        return 0

    lax.fori_loop(0, CHUNKS, drain, 0)


def body(spectra, w_embed, w_query, w_key, w_value, w_out, norm_gains, w_gate, w_up, w_down, w_head):
    vmem, dma = pltpu.VMEM, pltpu.SemaphoreType.DMA
    hbm = pl.BlockSpec(memory_space=pl.ANY)
    near = pl.BlockSpec(memory_space=pltpu.VMEM)
    result = pl.pallas_call(
        kernel,
        out_shape=jax.ShapeDtypeStruct((CHUNKS, ROWS, 2 * SLOTS), BF),
        in_specs=[hbm] * 8 + [near] + [hbm] * 4,
        out_specs=near,
        scratch_shapes=[
            vmem((2, 4, 2, 256, 384), BF),
            vmem((768, 512), BF),
            vmem((768, 512), BF),
            vmem((512, 512), BF),
            vmem((2 * SLOTS, D), BF),
            vmem((D, D), BF),
            vmem((D, D), BF),
            vmem((D, D), BF),
            vmem((D, D), BF),
            vmem((D, FF), BF),
            vmem((D, FF), BF),
            vmem((FF, D), BF),
            vmem((D, 2 * SLOTS), BF),
            vmem((CHUNKS, YN, XN, HALF, 128), BF),
            vmem((CHUNKS, XN, YN, HALF, 128), BF),
            vmem((CHUNKS, YN - 1, XN, HALF, 128), BF),
            vmem((CHUNKS, YN, HALF, 128), BF),
            vmem((CHUNKS, XN, HALF, 128), BF),
            vmem((CHUNKS, YN, HALF, 128), BF),
            vmem((CHUNKS, HALF, 128), BF),
            vmem((CHUNKS, YN - 1, HALF, 128), BF),
            vmem((CHUNKS, TM, 16, 128), BF),
            vmem((CHUNKS, TM, 16, 128), BF),
            vmem((ROWS, 128), F32),
            vmem((ROWS, 128), BF),
            vmem((ROWS, D), BF),
            vmem((ROWS, D), BF),
            vmem((ROWS, D), BF),
            vmem((ROWS, FF), BF),
            dma((14,)),
            dma((5, CHUNKS)),
            dma((5, CHUNKS)),
            pltpu.SemaphoreType.REGULAR((2,)),
        ],
        compiler_params=pltpu.CompilerParams(collective_id=0, has_side_effects=True, vmem_limit_bytes=58 << 20),
        name="fused",
    )(
        spectra, jnp.asarray(delay_tables()), jnp.asarray(doppler_tables()),
        w_embed, w_query, w_key, w_value, w_out, norm_gains, w_gate, w_up, w_down, w_head,
    )
    return result.reshape(2, 16, TILE, 2 * SLOTS)


def solution(mesh):
    placed = (P(None, "tm", None, None, "freq"), P(), P(), P(), P(), P(), P(), P(), P(), P(), P())
    return jax.shard_map(
        body, mesh=mesh, in_specs=placed, out_specs=P(None, "tm", "freq", None), check_vma=False
    )
```

```python
import math

import jax
import jax.numpy as jnp
import ml_dtypes
import numpy as np
from jax import lax
from jax.experimental import pallas as pl
from jax.experimental.pallas import tpu as pltpu
from jax.sharding import PartitionSpec as P

BF = jnp.bfloat16
F32 = jnp.float32
MESH = pl.DeviceIdType.MESH

SUBCARRIERS = 3072
TAPS = 256
SLOTS = 64
TILE = 32
FREQ = 8
XN, YN = 2, 4
TM = 16
D = 1024
HEADS = 8
FF = 2048
CHUNKS = 4
ROWS = 256
BLOCK = 128
HALF = ROWS // 2


def dot(a, b):
    return jnp.dot(a, b, preferred_element_type=F32)


def dot_t(a, b):
    return lax.dot_general(a, b, (((1,), (1,)), ((), ())), preferred_element_type=F32)


def delay_tables():
    share = SUBCARRIERS // FREQ
    f = np.arange(SUBCARRIERS)[:, None]
    t = np.arange(TAPS)[None, :]
    angle = 2.0 * math.pi / SUBCARRIERS * (f * t % SUBCARRIERS)
    r = 1.0 / math.sqrt(SUBCARRIERS)
    cosine, sine = np.cos(angle) * r, np.sin(angle) * r
    table = np.stack([np.stack([cosine, -sine], 1), np.stack([sine, cosine], 1)], 0)
    table = table.reshape(2, FREQ, share, 2, XN, YN, TILE)
    table = table.transpose(1, 0, 2, 5, 4, 3, 6)
    both = np.stack([table, table[:, :, :, :, ::-1]], 0)
    return both.reshape(2, FREQ, 2 * share, 2 * TAPS).astype(ml_dtypes.bfloat16)


def doppler_tables():
    s = np.arange(SLOTS)[:, None]
    k = np.arange(SLOTS)[None, :]
    angle = 2.0 * math.pi / SLOTS * (s * k % SLOTS)
    r = 1.0 / math.sqrt(SLOTS)
    cosine, sine = np.cos(angle) * r, np.sin(angle) * r
    table = np.stack([np.stack([cosine, -sine], 1), np.stack([sine, cosine], 1)], 0)
    table = table.reshape(2, TM, 2, 2, 2 * SLOTS)
    table = table.transpose(3, 0, 1, 2, 4)
    out = np.zeros((XN, 2, 2, 4, TM, 2, 4, 2 * SLOTS))
    for a in range(4):
        out[0, :, :, a, :, :, a] = table
        out[1, :, :, a, :, :, a] = table[::-1]
    return out.reshape(XN, 512, 512).astype(ml_dtypes.bfloat16)


def normed(x):
    return x * lax.rsqrt(jnp.mean(x * x, axis=-1, keepdims=True) + 1e-05)


def kernel(
    spectra, tables, doppler, w_embed, w_query, w_key, w_value, w_out, gains, w_gate, w_up, w_down, w_head,
    out,
    spec, tab_a, tab_b, dop, ve, vq, vk, vv, vo, vg, vu, vd, vh,
    part_a, part_b, got_a, got_b, sum_a, sum_b, last_a, last_b, taps, tiles, wide, feats, xs, hs, ms, hid,
    weg, pq, pk, pv, score_map, value_map, load_sem, sends, recvs, meet,
):
    freq = lax.axis_index("freq")
    tm = lax.axis_index("tm")
    mx, my = lax.div(freq, YN), lax.rem(freq, YN)

    loads = [
        (tables.at[0, freq], tab_a),
        (tables.at[1, freq], tab_b),
        (spectra.at[0], spec.at[0]),
        (spectra.at[1], spec.at[1]),
        (doppler.at[mx], dop),
        (w_embed, ve),
        (w_query.at[0], vq),
        (w_key.at[0], vk),
        (w_value.at[0], vv),
        (w_out.at[0], vo),
        (w_gate.at[0], vg),
        (w_up.at[0], vu),
        (w_down.at[0], vd),
        (w_head, vh),
    ]
    loads = [pltpu.make_async_copy(a, b, load_sem.at[i]) for i, (a, b) in enumerate(loads)]
    for load in loads[:3]:
        load.start()

    other_x = (1 - mx) * YN + my

    def along_y(i):
        return lax.rem(my + 1 + i, YN)

    tz, th, tc = lax.div(tm, 4), lax.rem(lax.div(tm, 2), 2), lax.rem(tm, 2)
    other_h = tz * 4 + (1 - th) * 2 + tc
    other_c = tz * 4 + th * 2 + (1 - tc)
    barrier = pltpu.get_barrier_semaphore()
    for i in range(YN - 1):
        pl.semaphore_signal(barrier, inc=1, device_id={"freq": mx * YN + along_y(i)}, device_id_type=MESH)
    pl.semaphore_signal(barrier, inc=1, device_id={"freq": other_x}, device_id_type=MESH)
    for i in range(1, 4):
        pl.semaphore_signal(barrier, inc=1, device_id={"tm": lax.rem(tm + 4 * i, TM)}, device_id_type=MESH)
    for other in (other_h, other_c):
        pl.semaphore_signal(barrier, inc=1, device_id={"tm": other}, device_id_type=MESH)

    low = lax.broadcasted_iota(jnp.int32, (ROWS, 128), 1) < 64

    def transform(u):
        for yp in range(2):
            cols = slice(256 * yp, 256 * yp + 256)
            sums = []
            for s in range(4):
                x = jnp.concatenate([spec[u, s, 0], spec[u, s, 1]], axis=1)
                sums.append(dot(x, (tab_b if s % 2 else tab_a)[:, cols]))
            for yy in range(2):
                a = [v[:, 128 * yy : 128 * yy + 128] for v in sums]
                for x in range(XN):
                    pair = [jnp.where(low, a[2 * sp + x], a[2 * sp + 1 - x]) for sp in range(2)]
                    pair = [v.reshape(TM, 2, 8, 128) for v in pair]
                    for ah in range(2):
                        rows = jnp.stack([pair[0][:, ah], pair[1][:, ah]], axis=1).reshape(ROWS, 128)
                        part_a[2 * u + ah, 2 * yp + yy, x] = rows[:HALF].astype(BF)
                        part_b[2 * u + ah, x, 2 * yp + yy] = rows[HALF:].astype(BF)

    def remote(src, dst, kind, c, device):
        return pltpu.make_async_remote_copy(
            src_ref=src,
            dst_ref=dst,
            send_sem=sends.at[kind, c],
            recv_sem=recvs.at[kind, c],
            device_id=device,
            device_id_type=MESH,
        )

    near_x = {"freq": other_x}

    def copy_a(c, i):
        y = along_y(i)
        return remote(part_a.at[c, y], got_a.at[c, i], 0, c, {"freq": mx * YN + y})

    def copy_b(c):
        return remote(part_b.at[c, 1 - mx], got_b.at[c], 1, c, near_x)

    def copy_sum_a(c):
        return remote(sum_a.at[c, 1 - mx], last_a.at[c], 2, c, near_x)

    def copy_sum_b(c, i):
        y = along_y(i)
        return remote(sum_b.at[c, y], last_b.at[c, i], 3, c, {"freq": mx * YN + y})

    def all_a(c):
        return remote(part_a.at[c, pl.ds(0, YN - 1)], got_a.at[c], 0, c, near_x)

    def all_sum_b(c):
        return remote(sum_b.at[c, pl.ds(0, YN - 1)], last_b.at[c], 3, c, near_x)

    def start_parts(c):
        copy_b(c).start()
        for i in (1, 0, 2):
            copy_a(c, i).start()

    def middle(c):
        all_a(c).wait_recv()
        for x in range(XN):
            total = part_a[c, my, x].astype(F32)
            for i in range(YN - 1):
                total = total + got_a[c, i, x].astype(F32)
            sum_a[c, x] = total.astype(BF)
        copy_sum_a(c).start()
        copy_b(c).wait_recv()
        for y in range(YN):
            sum_b[c, y] = (part_b[c, mx, y].astype(F32) + got_b[c, y].astype(F32)).astype(BF)
        for i in (1, 0, 2):
            copy_sum_b(c, i).start()

    def copy_tile(c, i):
        target = lax.rem(tm + i, TM)
        return remote(taps.at[c, target], tiles.at[c, tm], 4, c, {"tm": target})

    def all_tiles(c):
        return remote(taps.at[c, pl.ds(0, TM - 1)], tiles.at[c, pl.ds(0, TM - 1)], 4, c, {"tm": other_c})

    for load in loads[:3]:
        load.wait()
    for load in loads[3:]:
        load.start()
    transform(0)
    pl.semaphore_wait(barrier, 9)
    start_parts(0)
    pl.semaphore_signal(meet.at[0], inc=1, device_id={"tm": other_h}, device_id_type=MESH)
    loads[3].wait()
    transform(1)
    pl.semaphore_wait(meet.at[0], 1)
    pl.semaphore_signal(meet.at[1], inc=1, device_id={"tm": other_c}, device_id_type=MESH)
    pl.semaphore_wait(meet.at[1], 1)

    def reduce(c):
        copy_sum_a(c).wait_recv()
        taps[c, 0:8] = (sum_a[c, mx].astype(F32) + last_a[c].astype(F32)).astype(BF).reshape(TM // 2, 16, 128)
        all_sum_b(c).wait_recv()
        total = sum_b[c, my].astype(F32)
        for i in range(YN - 1):
            total = total + last_b[c, i].astype(F32)
        taps[c, 8:16] = total.astype(BF).reshape(TM // 2, 16, 128)

        def send(i, _):
            copy_tile(c, i).start()
            return 0

        lax.fori_loop(1, TM, send, 0)
        tiles[c, tm] = taps[c, tm]

    def parts_left(c):
        all_a(c).wait_send()
        copy_b(c).wait_send()

    def fold_inputs():
        for load in loads[5:9]:
            load.wait()
        weg[...] = (ve[...].astype(F32) * gains[0, 0:1, :]).astype(BF)
        for n in range(0, D, 256):
            cols = slice(n, n + 256)
            pq[:, cols] = dot(weg[...], vq[:, cols]).astype(BF)
            pk[:, cols] = dot(weg[...], vk[:, cols]).astype(BF)
            pv[:, cols] = dot(weg[...], vv[:, cols]).astype(BF)

    def fold_heads():
        loads[9].wait()
        for h in range(HEADS):
            cols = slice(h * 128, h * 128 + 128)
            score_map[:, cols] = dot_t(pq[:, cols], pk[:, cols]).astype(BF)
            value_map[cols, :] = dot(pv[:, cols], vo[cols, :]).astype(BF)

    parts_left(0)
    start_parts(1)
    middle(0)
    parts_left(1)
    start_parts(2)
    reduce(0)
    fold_inputs()
    middle(1)
    parts_left(2)
    start_parts(3)
    fold_heads()
    middle(2)
    reduce(1)
    loads[4].wait()
    for load in loads[10:]:
        load.wait()

    same_tile = (
        lax.broadcasted_iota(jnp.int32, (BLOCK, BLOCK), 0) // TILE
        == lax.broadcasted_iota(jnp.int32, (BLOCK, BLOCK), 1) // TILE
    )
    def doppler_of(c):
        all_tiles(c).wait_recv()
        wide[...] = tiles[c].astype(F32).reshape(ROWS, 128)
        groups = []
        for g in range(2):
            stacked = jnp.concatenate([wide[pl.ds(4 * g + a, 32, stride=8), :] for a in range(4)], axis=0)
            turned = stacked.T.astype(BF)
            groups.append(jnp.concatenate([turned[32 * q : 32 * q + 32] for q in range(4)], axis=1))
        spread = dot(jnp.concatenate(groups, axis=0), dop[...]).astype(BF)
        for g in range(2):
            for a in range(4):
                first = 32 * (4 * g + a)
                feats[first : first + 32, :] = spread[32 * g : 32 * g + 32, 128 * a : 128 * a + 128]

    def norm_rows(gain):
        for r in range(0, ROWS, 64):
            rows = slice(r, r + 64)
            value = normed(xs[rows, :].astype(F32))
            hs[rows, :] = (value if gain is None else value * gains[0, gain : gain + 1, :]).astype(BF)

    def attend(heads, scores, both):
        halves = [jnp.where(same_tile, v, -1e30) for s in scores for v in (s[:, :BLOCK], s[:, BLOCK:])]
        tops = [jnp.max(s, axis=-1, keepdims=True) for s in halves]
        weights = [jnp.exp((s - m) * 128**-0.5) for s, m in zip(halves, tops)]
        sums = [jnp.sum(p, axis=-1, keepdims=True) for p in weights]
        weights = [(p * (1.0 / t)).astype(BF) for p, t in zip(weights, sums)]
        for i, h in enumerate(heads):
            mixed = dot(jnp.concatenate(weights[2 * i : 2 * i + 2], axis=1), both).astype(BF)
            ms[:BLOCK, h * 128 : h * 128 + 128] = mixed[:, :128]
            ms[BLOCK:, h * 128 : h * 128 + 128] = mixed[:, 128:]

    def chunk(c, _):
        doppler_of(c)
        for n in range(0, D, 256):
            cols = slice(n, n + 256)
            xs[:, cols] = dot(feats[...], ve[:, cols]).astype(BF)
        squares = None
        for n in range(0, D, 128):
            v = xs[:, n : n + 128].astype(F32)
            squares = v * v if squares is None else squares + v * v
        factor = lax.rsqrt(jnp.sum(squares, axis=-1, keepdims=True) * (1.0 / D) + 1e-05)
        scaled = (feats[...].astype(F32) * factor).astype(BF)
        for n in range(0, D, 256):
            cols = slice(n, n + 256)
            hs[:, cols] = dot(scaled, score_map[:, cols]).astype(BF)
        zero = jnp.zeros((BLOCK, 128), BF)
        both = jnp.concatenate(
            [
                jnp.concatenate([scaled[:BLOCK], zero], axis=1),
                jnp.concatenate([zero, scaled[BLOCK:]], axis=1),
            ],
            axis=0,
        )
        waiting = []
        for first in range(0, HEADS, 2):
            heads, scores = (first, first + 1), []
            for h in heads:
                cols = slice(h * 128, h * 128 + 128)
                scores.append(dot_t(jnp.concatenate([hs[:BLOCK, cols], hs[BLOCK:, cols]], axis=1), both))
            waiting.append((heads, scores))
            if first:
                attend(*waiting.pop(0), both)
        attend(*waiting.pop(0), both)

        pl.when(c < CHUNKS - 2)(lambda: reduce(c + 2))

        for n in range(0, D, 256):
            cols = slice(n, n + 256)
            xs[:, cols] = (xs[:, cols].astype(F32) + dot(ms[...], value_map[:, cols])).astype(BF)

        pl.when(c < CHUNKS - 3)(lambda: middle(c + 3))

        norm_rows(1)
        for n in range(0, FF, 256):
            cols = slice(n, n + 256)
            gate = dot(hs[...], vg[:, cols])
            up = dot(hs[...], vu[:, cols])
            hid[:, cols] = (jax.nn.silu(gate) * up).astype(BF)
        for n in range(0, D, 256):
            cols = slice(n, n + 256)
            xs[:, cols] = (xs[:, cols].astype(F32) + dot(hid[...], vd[:, cols])).astype(BF)
        norm_rows(None)
        out[c] = dot(hs[...], vh[...]).astype(BF)
        return 0

    lax.fori_loop(0, CHUNKS, chunk, 0)

    def drain(c, _):
        copy_sum_a(c).wait_send()
        all_sum_b(c).wait_send()
        all_tiles(c).wait_send()
        return 0

    parts_left(CHUNKS - 1)
    lax.fori_loop(0, CHUNKS, drain, 0)


def body(spectra, w_embed, w_query, w_key, w_value, w_out, norm_gains, w_gate, w_up, w_down, w_head):
    vmem, dma = pltpu.VMEM, pltpu.SemaphoreType.DMA
    hbm = pl.BlockSpec(memory_space=pl.ANY)
    near = pl.BlockSpec(memory_space=pltpu.VMEM)
    result = pl.pallas_call(
        kernel,
        out_shape=jax.ShapeDtypeStruct((CHUNKS, ROWS, 2 * SLOTS), BF),
        in_specs=[hbm] * 8 + [near] + [hbm] * 4,
        out_specs=near,
        scratch_shapes=[
            vmem((2, 4, 2, 256, 384), BF),
            vmem((768, 512), BF),
            vmem((768, 512), BF),
            vmem((512, 512), BF),
            vmem((2 * SLOTS, D), BF),
            vmem((D, D), BF),
            vmem((D, D), BF),
            vmem((D, D), BF),
            vmem((D, D), BF),
            vmem((D, FF), BF),
            vmem((D, FF), BF),
            vmem((FF, D), BF),
            vmem((D, 2 * SLOTS), BF),
            vmem((CHUNKS, YN, XN, HALF, 128), BF),
            vmem((CHUNKS, XN, YN, HALF, 128), BF),
            vmem((CHUNKS, YN - 1, XN, HALF, 128), BF),
            vmem((CHUNKS, YN, HALF, 128), BF),
            vmem((CHUNKS, XN, HALF, 128), BF),
            vmem((CHUNKS, YN, HALF, 128), BF),
            vmem((CHUNKS, HALF, 128), BF),
            vmem((CHUNKS, YN - 1, HALF, 128), BF),
            vmem((CHUNKS, TM, 16, 128), BF),
            vmem((CHUNKS, TM, 16, 128), BF),
            vmem((ROWS, 128), F32),
            vmem((ROWS, 128), BF),
            vmem((ROWS, D), BF),
            vmem((ROWS, D), BF),
            vmem((ROWS, D), BF),
            vmem((ROWS, FF), BF),
            vmem((2 * SLOTS, D), BF),
            vmem((2 * SLOTS, D), BF),
            vmem((2 * SLOTS, D), BF),
            vmem((2 * SLOTS, D), BF),
            vmem((2 * SLOTS, D), BF),
            vmem((D, D), BF),
            dma((14,)),
            dma((5, CHUNKS)),
            dma((5, CHUNKS)),
            pltpu.SemaphoreType.REGULAR((2,)),
        ],
        compiler_params=pltpu.CompilerParams(collective_id=0, has_side_effects=True, vmem_limit_bytes=58 << 20),
        name="fused",
    )(
        spectra, jnp.asarray(delay_tables()), jnp.asarray(doppler_tables()),
        w_embed, w_query, w_key, w_value, w_out, norm_gains, w_gate, w_up, w_down, w_head,
    )
    return result.reshape(2, 16, TILE, 2 * SLOTS)


def solution(mesh):
    placed = (P(None, "tm", None, None, "freq"), P(), P(), P(), P(), P(), P(), P(), P(), P(), P())
    return jax.shard_map(
        body, mesh=mesh, in_specs=placed, out_specs=P(None, "tm", "freq", None), check_vma=False
    )
```

```python
import functools
import math

import jax
import jax.numpy as jnp
import ml_dtypes
import numpy as np
from jax import lax
from jax.experimental import pallas as pl
from jax.experimental.pallas import tpu as pltpu
from jax.sharding import PartitionSpec as P

BF = jnp.bfloat16
F32 = jnp.float32
MESH = pl.DeviceIdType.MESH

SUBCARRIERS = 3072
TAPS = 256
SLOTS = 64
TILE = 32
FREQ = 8
XN, YN = 2, 4
TM = 16
D = 1024
HEADS = 8
SCORE_SCALE = 128**-0.5 * math.log2(math.e)
FF = 2048
CHUNKS = 4
ROWS = 256
BLOCK = 128
HALF = ROWS // 2


def dot(a, b):
    return jnp.dot(a, b, preferred_element_type=F32)


def dot_t(a, b):
    return lax.dot_general(a, b, (((1,), (1,)), ((), ())), preferred_element_type=F32)


def delay_tables():
    share = SUBCARRIERS // FREQ
    f = np.arange(SUBCARRIERS)[:, None]
    t = np.arange(TAPS)[None, :]
    angle = 2.0 * math.pi / SUBCARRIERS * (f * t % SUBCARRIERS)
    r = 1.0 / math.sqrt(SUBCARRIERS)
    cosine, sine = np.cos(angle) * r, np.sin(angle) * r
    table = np.stack([np.stack([cosine, -sine], 1), np.stack([sine, cosine], 1)], 0)
    table = table.reshape(2, FREQ, share, 2, XN, YN, TILE)
    table = table.transpose(1, 0, 2, 5, 4, 3, 6)
    both = np.stack([table, table[:, :, :, :, ::-1]], 0)
    return both.reshape(2, FREQ, 2 * share, 2 * TAPS).astype(ml_dtypes.bfloat16)


def doppler_tables():
    s = np.arange(SLOTS)[:, None]
    k = np.arange(SLOTS)[None, :]
    angle = 2.0 * math.pi / SLOTS * (s * k % SLOTS)
    r = 1.0 / math.sqrt(SLOTS)
    cosine, sine = np.cos(angle) * r, np.sin(angle) * r
    table = np.stack([np.stack([cosine, -sine], 1), np.stack([sine, cosine], 1)], 0)
    table = table.reshape(2, TM, 2, 2, 2 * SLOTS)
    table = table.transpose(3, 0, 1, 2, 4)
    out = np.zeros((XN, 2, 2, 4, TM, 2, 4, 2 * SLOTS))
    for a in range(4):
        out[0, :, :, a, :, :, a] = table
        out[1, :, :, a, :, :, a] = table[::-1]
    return out.reshape(XN, 512, 512).astype(ml_dtypes.bfloat16)


def normed(x):
    return x * lax.rsqrt(jnp.mean(x * x, axis=-1, keepdims=True) + 1e-05)


def kernel(
    spectra, tables, doppler, w_embed, w_query, w_key, w_value, w_out, gains, w_gate, w_up, w_down, w_head,
    out,
    spec, tab_a, tab_b, dop, ve, vq, vk, vv, vo, vg, vu, vd, vh,
    part_a, part_b, got_a, got_b, sum_a, sum_b, last_a, last_b, taps, tiles, wide, feats, xs, hs, ms, hid, xb, h2, fin,
    weg, pq, pk, pv, score_map, value_map, load_sem, sends, recvs, meet,
):
    freq = lax.axis_index("freq")
    tm = lax.axis_index("tm")
    mx, my = lax.div(freq, YN), lax.rem(freq, YN)

    loads = [
        (tables.at[0, freq], tab_a),
        (tables.at[1, freq], tab_b),
        (spectra.at[0], spec.at[0]),
        (spectra.at[1], spec.at[1]),
        (doppler.at[mx], dop),
        (w_embed, ve),
        (w_query.at[0], vq),
        (w_key.at[0], vk),
        (w_value.at[0], vv),
        (w_out.at[0], vo),
        (w_gate.at[0], vg),
        (w_up.at[0], vu),
        (w_down.at[0], vd),
        (w_head, vh),
    ]
    loads = [pltpu.make_async_copy(a, b, load_sem.at[i]) for i, (a, b) in enumerate(loads)]
    for load in loads[:3]:
        load.start()

    other_x = (1 - mx) * YN + my

    def along_y(i):
        return lax.rem(my + 1 + i, YN)

    tz, th, tc = lax.div(tm, 4), lax.rem(lax.div(tm, 2), 2), lax.rem(tm, 2)
    other_h = tz * 4 + (1 - th) * 2 + tc
    other_c = tz * 4 + th * 2 + (1 - tc)
    barrier = pltpu.get_barrier_semaphore()
    for i in range(YN - 1):
        pl.semaphore_signal(barrier, inc=1, device_id={"freq": mx * YN + along_y(i)}, device_id_type=MESH)
    pl.semaphore_signal(barrier, inc=1, device_id={"freq": other_x}, device_id_type=MESH)
    for i in range(1, 4):
        pl.semaphore_signal(barrier, inc=1, device_id={"tm": lax.rem(tm + 4 * i, TM)}, device_id_type=MESH)
    for other in (other_h, other_c):
        pl.semaphore_signal(barrier, inc=1, device_id={"tm": other}, device_id_type=MESH)

    low = lax.broadcasted_iota(jnp.int32, (ROWS, 128), 1) < 64

    def transform(u):
        for yp in range(2):
            cols = slice(256 * yp, 256 * yp + 256)
            sums = []
            for s in range(4):
                x = jnp.concatenate([spec[u, s, 0], spec[u, s, 1]], axis=1)
                sums.append(dot(x, (tab_b if s % 2 else tab_a)[:, cols]))
            for yy in range(2):
                a = [v[:, 128 * yy : 128 * yy + 128] for v in sums]
                for x in range(XN):
                    pair = [jnp.where(low, a[2 * sp + x], a[2 * sp + 1 - x]) for sp in range(2)]
                    pair = [v.reshape(TM, 2, 8, 128) for v in pair]
                    for ah in range(2):
                        rows = jnp.stack([pair[0][:, ah], pair[1][:, ah]], axis=1).reshape(ROWS, 128)
                        part_a[2 * u + ah, 2 * yp + yy, x] = rows[:HALF].astype(BF)
                        part_b[2 * u + ah, x, 2 * yp + yy] = rows[HALF:].astype(BF)

    def remote(src, dst, kind, c, device):
        return pltpu.make_async_remote_copy(
            src_ref=src,
            dst_ref=dst,
            send_sem=sends.at[kind, c],
            recv_sem=recvs.at[kind, c],
            device_id=device,
            device_id_type=MESH,
        )

    near_x = {"freq": other_x}

    def copy_a(c, i):
        y = along_y(i)
        return remote(part_a.at[c, y], got_a.at[c, i], 0, c, {"freq": mx * YN + y})

    def copy_b(c):
        return remote(part_b.at[c, 1 - mx], got_b.at[c], 1, c, near_x)

    def copy_sum_a(c):
        return remote(sum_a.at[c, 1 - mx], last_a.at[c], 2, c, near_x)

    def copy_sum_b(c, i):
        y = along_y(i)
        return remote(sum_b.at[c, y], last_b.at[c, i], 3, c, {"freq": mx * YN + y})

    def all_a(c):
        return remote(part_a.at[c, pl.ds(0, YN - 1)], got_a.at[c], 0, c, near_x)

    def all_sum_b(c):
        return remote(sum_b.at[c, pl.ds(0, YN - 1)], last_b.at[c], 3, c, near_x)

    def start_parts(c):
        copy_b(c).start()
        for i in (1, 0, 2):
            copy_a(c, i).start()

    def middle(c):
        all_a(c).wait_recv()
        for x in range(XN):
            total = part_a[c, my, x].astype(F32)
            for i in range(YN - 1):
                total = total + got_a[c, i, x].astype(F32)
            sum_a[c, x] = total.astype(BF)
        copy_sum_a(c).start()
        copy_b(c).wait_recv()
        for y in range(YN):
            sum_b[c, y] = (part_b[c, mx, y].astype(F32) + got_b[c, y].astype(F32)).astype(BF)
        for i in (1, 0, 2):
            copy_sum_b(c, i).start()

    def copy_tile(c, i):
        target = lax.rem(tm + i, TM)
        return remote(taps.at[c, target], tiles.at[c, tm], 4, c, {"tm": target})

    def all_tiles(c):
        return remote(taps.at[c, pl.ds(0, TM - 1)], tiles.at[c, pl.ds(0, TM - 1)], 4, c, {"tm": other_c})

    for load in loads[:3]:
        load.wait()
    for load in loads[3:]:
        load.start()
    transform(0)
    pl.semaphore_wait(barrier, 9)
    start_parts(0)
    pl.semaphore_signal(meet.at[0], inc=1, device_id={"tm": other_h}, device_id_type=MESH)
    loads[3].wait()
    transform(1)
    pl.semaphore_wait(meet.at[0], 1)
    pl.semaphore_signal(meet.at[1], inc=1, device_id={"tm": other_c}, device_id_type=MESH)
    pl.semaphore_wait(meet.at[1], 1)

    def reduce(c):
        copy_sum_a(c).wait_recv()
        taps[c, 0:8] = (sum_a[c, mx].astype(F32) + last_a[c].astype(F32)).astype(BF).reshape(TM // 2, 16, 128)
        all_sum_b(c).wait_recv()
        total = sum_b[c, my].astype(F32)
        for i in range(YN - 1):
            total = total + last_b[c, i].astype(F32)
        taps[c, 8:16] = total.astype(BF).reshape(TM // 2, 16, 128)

        def send(i, _):
            copy_tile(c, i).start()
            return 0

        lax.fori_loop(1, TM, send, 0)
        tiles[c, tm] = taps[c, tm]

    def parts_left(c):
        all_a(c).wait_send()
        copy_b(c).wait_send()

    def fold_inputs():
        for load in loads[5:9]:
            load.wait()
        weg[...] = (ve[...].astype(F32) * gains[0, 0:1, :]).astype(BF)
        for n in range(0, D, 256):
            cols = slice(n, n + 256)
            pq[:, cols] = dot(weg[...], vq[:, cols]).astype(BF)
            pk[:, cols] = dot(weg[...], vk[:, cols]).astype(BF)
            pv[:, cols] = dot(weg[...], vv[:, cols]).astype(BF)

    def fold_heads():
        loads[9].wait()
        for h in range(HEADS):
            cols = slice(h * 128, h * 128 + 128)
            score_map[:, cols] = (dot_t(pq[:, cols], pk[:, cols]) * SCORE_SCALE).astype(BF)
            value_map[cols, :] = dot(pv[:, cols], vo[cols, :]).astype(BF)

    parts_left(0)
    start_parts(1)
    middle(0)
    parts_left(1)
    start_parts(2)
    reduce(0)
    middle(1)
    parts_left(2)
    start_parts(3)
    fold_inputs()
    fold_heads()
    reduce(1)
    loads[4].wait()
    for load in loads[10:]:
        load.wait()

    same_tile = (
        lax.broadcasted_iota(jnp.int32, (BLOCK, BLOCK), 0) // TILE
        == lax.broadcasted_iota(jnp.int32, (BLOCK, BLOCK), 1) // TILE
    )
    def doppler_of(c):
        all_tiles(c).wait_recv()
        wide[...] = tiles[c].astype(F32).reshape(ROWS, 128)
        groups = []
        for g in range(2):
            stacked = jnp.concatenate([wide[pl.ds(4 * g + a, 32, stride=8), :] for a in range(4)], axis=0)
            turned = stacked.T.astype(BF)
            groups.append(jnp.concatenate([turned[32 * q : 32 * q + 32] for q in range(4)], axis=1))
        spread = dot(jnp.concatenate(groups, axis=0), dop[...]).astype(BF)
        for g in range(2):
            for a in range(4):
                first = 32 * (4 * g + a)
                feats[first : first + 32, :] = spread[32 * g : 32 * g + 32, 128 * a : 128 * a + 128]

    def interleave(*lists):
        steps = [((n + 0.5) / len(one), k, step) for k, one in enumerate(lists) for n, step in enumerate(one)]
        for _, _, step in sorted(steps, key=lambda entry: entry[:2]):
            step()

    def norm_steps(target, read, gain):
        def step(first):
            rows = slice(first, first + 64)
            value = normed(read(rows).astype(F32))
            target[rows, :] = (value if gain is None else value * gains[0, gain : gain + 1, :]).astype(BF)

        return [functools.partial(step, first) for first in range(0, ROWS, 64)]

    def enter(c):
        doppler_of(c)
        squares = None
        for n in range(0, D, 256):
            cols = slice(n, n + 256)
            x = dot(feats[...], ve[:, cols]).astype(BF)
            xs[:, cols] = x
            v = x.astype(F32)
            v = v * v
            v = v[:, :128] + v[:, 128:]
            squares = v if squares is None else squares + v
        factor = lax.rsqrt(jnp.sum(squares, axis=-1, keepdims=True) * (1.0 / D) + 1e-05)
        scaled = (feats[...].astype(F32) * factor).astype(BF)
        for n in range(0, D, 256):
            cols = slice(n, n + 256)
            hs[:, cols] = dot(scaled, score_map[:, cols]).astype(BF)
        zero = jnp.zeros((BLOCK, 128), BF)
        return jnp.concatenate(
            [
                jnp.concatenate([scaled[:BLOCK], zero], axis=1),
                jnp.concatenate([zero, scaled[BLOCK:]], axis=1),
            ],
            axis=0,
        )

    def attention_steps(both):
        held = {}

        def score(h):
            cols = slice(h * 128, h * 128 + 128)
            held[h] = dot_t(jnp.concatenate([hs[:BLOCK, cols], hs[BLOCK:, cols]], axis=1), both)

        def top(h):
            halves = [jnp.where(same_tile, v, -1e30) for v in (held[h][:, :BLOCK], held[h][:, BLOCK:])]
            held[h] = [v - jnp.max(v, axis=-1, keepdims=True) for v in halves]

        def power(h):
            weights = [jnp.exp2(v) for v in held[h]]
            sums = [jnp.sum(p, axis=-1, keepdims=True) for p in weights]
            held[h] = (jnp.concatenate([p.astype(BF) for p in weights], axis=1), [1.0 / t for t in sums])

        def mix(h):
            weights, factors = held.pop(h)
            mixed = dot(weights, both)
            cols = slice(h * 128, h * 128 + 128)
            ms[:BLOCK, cols] = (mixed[:, :128] * factors[0]).astype(BF)
            ms[BLOCK:, cols] = (mixed[:, 128:] * factors[1]).astype(BF)

        steps = []
        for pair in range(HEADS // 2 + 1):
            for kind, back in ((score, 0), (top, 1), (power, 1), (mix, 1)):
                for h in (2 * (pair - back), 2 * (pair - back) + 1):
                    if 0 <= h < HEADS:
                        steps.append(functools.partial(kind, h))
        return steps

    def leave_attention(slot):
        for n in range(0, D, 256):
            cols = slice(n, n + 256)
            xb[slot, :, cols] = (xs[:, cols].astype(F32) + dot(ms[...], value_map[:, cols])).astype(BF)

    def gate_steps():
        def step(n):
            cols = slice(n, n + 256)
            gate = dot(h2[...], vg[:, cols])
            up = dot(h2[...], vu[:, cols])
            hid[:, cols] = (jax.nn.silu(gate) * up).astype(BF)

        return [functools.partial(step, n) for n in range(0, FF, 256)]

    def down_steps(slot):
        def step(n):
            cols = slice(n, n + 256)
            fin[:, cols] = (xb[slot, :, cols].astype(F32) + dot(hid[...], vd[:, cols])).astype(BF)

        return [functools.partial(step, n) for n in range(0, D, 256)]

    def finish(c):
        interleave(norm_steps(hs, lambda rows: fin[rows, :], None))
        out[c] = dot(hs[...], vh[...]).astype(BF)

    interleave(attention_steps(enter(0)))
    middle(2)
    leave_attention(0)
    interleave(norm_steps(h2, lambda rows: xb[0, rows, :], 1))

    def chunk(c, _):
        slot = lax.rem(c, 2)
        pl.when(c < CHUNKS - 3)(lambda: middle(c + 3))
        gates = gate_steps()
        interleave(gates[:4])
        both = enter(c + 1)
        pl.when(c < CHUNKS - 2)(lambda: reduce(c + 2))
        interleave(attention_steps(both), gates[4:])
        leave_attention(1 - slot)
        interleave(down_steps(slot), norm_steps(h2, lambda rows: xb[1 - slot, rows, :], 1))
        finish(c)
        return 0

    lax.fori_loop(0, CHUNKS - 1, chunk, 0)
    interleave(gate_steps())
    interleave(down_steps((CHUNKS - 1) % 2))
    finish(CHUNKS - 1)

    def drain(c, _):
        copy_sum_a(c).wait_send()
        all_sum_b(c).wait_send()
        all_tiles(c).wait_send()
        return 0

    parts_left(CHUNKS - 1)
    lax.fori_loop(0, CHUNKS, drain, 0)


def body(spectra, w_embed, w_query, w_key, w_value, w_out, norm_gains, w_gate, w_up, w_down, w_head):
    vmem, dma = pltpu.VMEM, pltpu.SemaphoreType.DMA
    hbm = pl.BlockSpec(memory_space=pl.ANY)
    near = pl.BlockSpec(memory_space=pltpu.VMEM)
    result = pl.pallas_call(
        kernel,
        out_shape=jax.ShapeDtypeStruct((CHUNKS, ROWS, 2 * SLOTS), BF),
        in_specs=[hbm] * 8 + [near] + [hbm] * 4,
        out_specs=near,
        scratch_shapes=[
            vmem((2, 4, 2, 256, 384), BF),
            vmem((768, 512), BF),
            vmem((768, 512), BF),
            vmem((512, 512), BF),
            vmem((2 * SLOTS, D), BF),
            vmem((D, D), BF),
            vmem((D, D), BF),
            vmem((D, D), BF),
            vmem((D, D), BF),
            vmem((D, FF), BF),
            vmem((D, FF), BF),
            vmem((FF, D), BF),
            vmem((D, 2 * SLOTS), BF),
            vmem((CHUNKS, YN, XN, HALF, 128), BF),
            vmem((CHUNKS, XN, YN, HALF, 128), BF),
            vmem((CHUNKS, YN - 1, XN, HALF, 128), BF),
            vmem((CHUNKS, YN, HALF, 128), BF),
            vmem((CHUNKS, XN, HALF, 128), BF),
            vmem((CHUNKS, YN, HALF, 128), BF),
            vmem((CHUNKS, HALF, 128), BF),
            vmem((CHUNKS, YN - 1, HALF, 128), BF),
            vmem((CHUNKS, TM, 16, 128), BF),
            vmem((CHUNKS, TM, 16, 128), BF),
            vmem((ROWS, 128), F32),
            vmem((ROWS, 128), BF),
            vmem((ROWS, D), BF),
            vmem((ROWS, D), BF),
            vmem((ROWS, D), BF),
            vmem((ROWS, FF), BF),
            vmem((2, ROWS, D), BF),
            vmem((ROWS, D), BF),
            vmem((ROWS, D), BF),
            vmem((2 * SLOTS, D), BF),
            vmem((2 * SLOTS, D), BF),
            vmem((2 * SLOTS, D), BF),
            vmem((2 * SLOTS, D), BF),
            vmem((2 * SLOTS, D), BF),
            vmem((D, D), BF),
            dma((14,)),
            dma((5, CHUNKS)),
            dma((5, CHUNKS)),
            pltpu.SemaphoreType.REGULAR((2,)),
        ],
        compiler_params=pltpu.CompilerParams(collective_id=0, has_side_effects=True, vmem_limit_bytes=58 << 20),
        name="fused",
    )(
        spectra, jnp.asarray(delay_tables()), jnp.asarray(doppler_tables()),
        w_embed, w_query, w_key, w_value, w_out, norm_gains, w_gate, w_up, w_down, w_head,
    )
    return result.reshape(2, 16, TILE, 2 * SLOTS)


def solution(mesh):
    placed = (P(None, "tm", None, None, "freq"), P(), P(), P(), P(), P(), P(), P(), P(), P(), P())
    return jax.shard_map(
        body, mesh=mesh, in_specs=placed, out_specs=P(None, "tm", "freq", None), check_vma=False
    )
```

```python
import functools
import math

import jax
import jax.numpy as jnp
import ml_dtypes
import numpy as np
from jax import lax
from jax.experimental import pallas as pl
from jax.experimental.pallas import tpu as pltpu
from jax.sharding import PartitionSpec as P

BF = jnp.bfloat16
F32 = jnp.float32
MESH = pl.DeviceIdType.MESH

SUBCARRIERS = 3072
TAPS = 256
SLOTS = 64
TILE = 32
FREQ = 8
XN, YN = 2, 4
TM = 16
D = 1024
HEADS = 8
SCORE_SCALE = 128**-0.5 * math.log2(math.e)
FF = 2048
CHUNKS = 4
ROWS = 256
BLOCK = 128
HALF = ROWS // 2


def dot(a, b):
    return jnp.dot(a, b, preferred_element_type=F32)


def dot_t(a, b):
    return lax.dot_general(a, b, (((1,), (1,)), ((), ())), preferred_element_type=F32)


def delay_tables():
    share = SUBCARRIERS // FREQ
    f = np.arange(SUBCARRIERS)[:, None]
    t = np.arange(TAPS)[None, :]
    angle = 2.0 * math.pi / SUBCARRIERS * (f * t % SUBCARRIERS)
    r = 1.0 / math.sqrt(SUBCARRIERS)
    cosine, sine = np.cos(angle) * r, np.sin(angle) * r
    table = np.stack([np.stack([cosine, -sine], 1), np.stack([sine, cosine], 1)], 0)
    table = table.reshape(2, FREQ, share, 2, XN, YN, TILE)
    table = table.transpose(1, 0, 2, 5, 4, 3, 6)
    both = np.stack([table, table[:, :, :, :, ::-1]], 0)
    return both.reshape(2, FREQ, 2 * share, 2 * TAPS).astype(ml_dtypes.bfloat16)


def doppler_tables():
    s = np.arange(SLOTS)[:, None]
    k = np.arange(SLOTS)[None, :]
    angle = 2.0 * math.pi / SLOTS * (s * k % SLOTS)
    r = 1.0 / math.sqrt(SLOTS)
    cosine, sine = np.cos(angle) * r, np.sin(angle) * r
    table = np.stack([np.stack([cosine, -sine], 1), np.stack([sine, cosine], 1)], 0)
    table = table.reshape(2, TM, 2, 2, 2 * SLOTS)
    table = table.transpose(3, 0, 1, 2, 4)
    out = np.zeros((XN, 2, 2, 4, TM, 2, 4, 2 * SLOTS))
    for a in range(4):
        out[0, :, :, a, :, :, a] = table
        out[1, :, :, a, :, :, a] = table[::-1]
    return out.reshape(XN, 512, 512).astype(ml_dtypes.bfloat16)


def normed(x):
    return x * lax.rsqrt(jnp.mean(x * x, axis=-1, keepdims=True) + 1e-05)


def kernel(
    spectra, tables, doppler, w_embed, w_query, w_key, w_value, w_out, gains, w_gate, w_up, w_down, w_head,
    out,
    spec, tab_a, tab_b, dop, ve, vq, vk, vv, vo, vg, vu, vd, vh,
    part_a, part_b, got_a, got_b, sum_a, sum_b, last_a, last_b, taps, tiles, wide, feats, xs, hs, ms, hid, xb, h2, fin,
    weg, pq, pk, pv, score_map, value_map, load_sem, sends, recvs, meet,
):
    freq = lax.axis_index("freq")
    tm = lax.axis_index("tm")
    mx, my = lax.div(freq, YN), lax.rem(freq, YN)

    loads = [
        (tables.at[0, freq], tab_a),
        (tables.at[1, freq], tab_b),
        (spectra.at[0], spec.at[0]),
        (spectra.at[1], spec.at[1]),
        (doppler.at[mx], dop),
        (w_embed, ve),
        (w_query.at[0], vq),
        (w_key.at[0], vk),
        (w_value.at[0], vv),
        (w_out.at[0], vo),
        (w_gate.at[0], vg),
        (w_up.at[0], vu),
        (w_down.at[0], vd),
        (w_head, vh),
    ]
    loads = [pltpu.make_async_copy(a, b, load_sem.at[i]) for i, (a, b) in enumerate(loads)]
    for load in loads[:3]:
        load.start()

    other_x = (1 - mx) * YN + my

    def along_y(i):
        return lax.rem(my + 1 + i, YN)

    tz, th, tc = lax.div(tm, 4), lax.rem(lax.div(tm, 2), 2), lax.rem(tm, 2)
    other_h = tz * 4 + (1 - th) * 2 + tc
    other_c = tz * 4 + th * 2 + (1 - tc)
    barrier = pltpu.get_barrier_semaphore()
    for i in range(YN - 1):
        pl.semaphore_signal(barrier, inc=1, device_id={"freq": mx * YN + along_y(i)}, device_id_type=MESH)
    pl.semaphore_signal(barrier, inc=1, device_id={"freq": other_x}, device_id_type=MESH)
    for i in range(1, 4):
        pl.semaphore_signal(barrier, inc=1, device_id={"tm": lax.rem(tm + 4 * i, TM)}, device_id_type=MESH)
    for other in (other_h, other_c):
        pl.semaphore_signal(barrier, inc=1, device_id={"tm": other}, device_id_type=MESH)

    low = lax.broadcasted_iota(jnp.int32, (ROWS, 128), 1) < 64

    def transform(u):
        for yp in range(2):
            cols = slice(256 * yp, 256 * yp + 256)
            sums = []
            for s in range(4):
                x = jnp.concatenate([spec[u, s, 0], spec[u, s, 1]], axis=1)
                sums.append(dot(x, (tab_b if s % 2 else tab_a)[:, cols]))
            for yy in range(2):
                a = [v[:, 128 * yy : 128 * yy + 128] for v in sums]
                for x in range(XN):
                    pair = [jnp.where(low, a[2 * sp + x], a[2 * sp + 1 - x]) for sp in range(2)]
                    pair = [v.reshape(TM, 2, 8, 128) for v in pair]
                    for ah in range(2):
                        rows = jnp.stack([pair[0][:, ah], pair[1][:, ah]], axis=1).reshape(ROWS, 128)
                        part_a[2 * u + ah, 2 * yp + yy, x] = rows[:HALF].astype(BF)
                        part_b[2 * u + ah, x, 2 * yp + yy] = rows[HALF:].astype(BF)

    def remote(src, dst, kind, c, device):
        return pltpu.make_async_remote_copy(
            src_ref=src,
            dst_ref=dst,
            send_sem=sends.at[kind, c],
            recv_sem=recvs.at[kind, c],
            device_id=device,
            device_id_type=MESH,
        )

    near_x = {"freq": other_x}

    def copy_a(c, i):
        y = along_y(i)
        return remote(part_a.at[c, y], got_a.at[c, i], 0, c, {"freq": mx * YN + y})

    def copy_b(c):
        return remote(part_b.at[c, 1 - mx], got_b.at[c], 1, c, near_x)

    def copy_sum_a(c):
        return remote(sum_a.at[c, 1 - mx], last_a.at[c], 2, c, near_x)

    def copy_sum_b(c, i):
        y = along_y(i)
        return remote(sum_b.at[c, y], last_b.at[c, i], 3, c, {"freq": mx * YN + y})

    def all_a(c):
        return remote(part_a.at[c, pl.ds(0, YN - 1)], got_a.at[c], 0, c, near_x)

    def all_sum_b(c):
        return remote(sum_b.at[c, pl.ds(0, YN - 1)], last_b.at[c], 3, c, near_x)

    def start_parts(c):
        copy_b(c).start()
        for i in (1, 0, 2):
            copy_a(c, i).start()

    def middle(c):
        all_a(c).wait_recv()
        for x in range(XN):
            total = part_a[c, my, x].astype(F32)
            for i in range(YN - 1):
                total = total + got_a[c, i, x].astype(F32)
            sum_a[c, x] = total.astype(BF)
        copy_sum_a(c).start()
        copy_b(c).wait_recv()
        for y in range(YN):
            sum_b[c, y] = (part_b[c, mx, y].astype(F32) + got_b[c, y].astype(F32)).astype(BF)
        for i in (1, 0, 2):
            copy_sum_b(c, i).start()

    def all_tiles(c):
        return remote(taps.at[c, pl.ds(0, TM - 1)], tiles.at[c, pl.ds(0, TM - 1)], 4, c, {"tm": other_c})

    for load in loads[:3]:
        load.wait()
    for load in loads[3:]:
        load.start()
    transform(0)
    pl.semaphore_wait(barrier, 9)
    start_parts(0)
    pl.semaphore_signal(meet.at[0], inc=1, device_id={"tm": other_h}, device_id_type=MESH)
    loads[3].wait()
    transform(1)
    pl.semaphore_wait(meet.at[0], 1)
    pl.semaphore_signal(meet.at[1], inc=1, device_id={"tm": other_c}, device_id_type=MESH)
    pl.semaphore_wait(meet.at[1], 1)

    def send_tiles(c, first):
        def send(t, _):
            @pl.when(t != tm)
            def _():
                remote(taps.at[c, t], tiles.at[c, tm], 4, c, {"tm": t}).start()

            return 0

        lax.fori_loop(first, first + TM // 2, send, 0)

    def reduce(c):
        copy_sum_a(c).wait_recv()
        taps[c, 0:8] = (sum_a[c, mx].astype(F32) + last_a[c].astype(F32)).astype(BF).reshape(TM // 2, 16, 128)
        send_tiles(c, 0)
        all_sum_b(c).wait_recv()
        total = sum_b[c, my].astype(F32)
        for i in range(YN - 1):
            total = total + last_b[c, i].astype(F32)
        taps[c, 8:16] = total.astype(BF).reshape(TM // 2, 16, 128)
        send_tiles(c, TM // 2)
        tiles[c, tm] = taps[c, tm]

    def parts_left(c):
        all_a(c).wait_send()
        copy_b(c).wait_send()

    def fold_inputs():
        for load in loads[5:9]:
            load.wait()
        weg[...] = (ve[...].astype(F32) * gains[0, 0:1, :]).astype(BF)
        for n in range(0, D, 256):
            cols = slice(n, n + 256)
            pq[:, cols] = dot(weg[...], vq[:, cols]).astype(BF)
            pk[:, cols] = dot(weg[...], vk[:, cols]).astype(BF)
            pv[:, cols] = dot(weg[...], vv[:, cols]).astype(BF)

    def fold_heads():
        loads[9].wait()
        for h in range(HEADS):
            cols = slice(h * 128, h * 128 + 128)
            score_map[:, cols] = (dot_t(pq[:, cols], pk[:, cols]) * SCORE_SCALE).astype(BF)
            value_map[cols, :] = dot(pv[:, cols], vo[cols, :]).astype(BF)

    parts_left(0)
    start_parts(1)
    middle(0)
    parts_left(1)
    start_parts(2)
    reduce(0)
    middle(1)
    parts_left(2)
    start_parts(3)
    fold_inputs()
    fold_heads()
    reduce(1)
    loads[4].wait()
    for load in loads[10:]:
        load.wait()

    same_tile = (
        lax.broadcasted_iota(jnp.int32, (BLOCK, BLOCK), 0) // TILE
        == lax.broadcasted_iota(jnp.int32, (BLOCK, BLOCK), 1) // TILE
    )
    def doppler_of(c):
        all_tiles(c).wait_recv()
        wide[...] = tiles[c].astype(F32).reshape(ROWS, 128)
        groups = []
        for g in range(2):
            stacked = jnp.concatenate([wide[pl.ds(4 * g + a, 32, stride=8), :] for a in range(4)], axis=0)
            turned = stacked.T.astype(BF)
            groups.append(jnp.concatenate([turned[32 * q : 32 * q + 32] for q in range(4)], axis=1))
        spread = dot(jnp.concatenate(groups, axis=0), dop[...]).astype(BF)
        for g in range(2):
            for a in range(4):
                first = 32 * (4 * g + a)
                feats[first : first + 32, :] = spread[32 * g : 32 * g + 32, 128 * a : 128 * a + 128]

    def interleave(*lists):
        steps = [((n + 0.5) / len(one), k, step) for k, one in enumerate(lists) for n, step in enumerate(one)]
        for _, _, step in sorted(steps, key=lambda entry: entry[:2]):
            step()

    def norm_steps(target, read, gain):
        def step(first):
            rows = slice(first, first + 64)
            value = normed(read(rows).astype(F32))
            target[rows, :] = (value if gain is None else value * gains[0, gain : gain + 1, :]).astype(BF)

        return [functools.partial(step, first) for first in range(0, ROWS, 64)]

    def enter(c):
        doppler_of(c)
        squares = None
        for n in range(0, D, 256):
            cols = slice(n, n + 256)
            x = dot(feats[...], ve[:, cols]).astype(BF)
            xs[:, cols] = x
            v = x.astype(F32)
            v = v * v
            v = v[:, :128] + v[:, 128:]
            squares = v if squares is None else squares + v
        factor = lax.rsqrt(jnp.sum(squares, axis=-1, keepdims=True) * (1.0 / D) + 1e-05)
        scaled = (feats[...].astype(F32) * factor).astype(BF)
        for n in range(0, D, 256):
            cols = slice(n, n + 256)
            hs[:, cols] = dot(scaled, score_map[:, cols]).astype(BF)
        zero = jnp.zeros((BLOCK, 128), BF)
        return jnp.concatenate(
            [
                jnp.concatenate([scaled[:BLOCK], zero], axis=1),
                jnp.concatenate([zero, scaled[BLOCK:]], axis=1),
            ],
            axis=0,
        )

    def attention_steps(both):
        held = {}

        def score(h):
            cols = slice(h * 128, h * 128 + 128)
            held[h] = dot_t(jnp.concatenate([hs[:BLOCK, cols], hs[BLOCK:, cols]], axis=1), both)

        def top(h):
            halves = [jnp.where(same_tile, v, -1e30) for v in (held[h][:, :BLOCK], held[h][:, BLOCK:])]
            held[h] = [v - jnp.max(v, axis=-1, keepdims=True) for v in halves]

        def power(h):
            weights = [jnp.exp2(v) for v in held[h]]
            sums = [jnp.sum(p, axis=-1, keepdims=True) for p in weights]
            held[h] = (jnp.concatenate([p.astype(BF) for p in weights], axis=1), [1.0 / t for t in sums])

        def mix(h):
            weights, factors = held.pop(h)
            mixed = dot(weights, both)
            cols = slice(h * 128, h * 128 + 128)
            ms[:BLOCK, cols] = (mixed[:, :128] * factors[0]).astype(BF)
            ms[BLOCK:, cols] = (mixed[:, 128:] * factors[1]).astype(BF)

        steps = []
        for pair in range(HEADS // 2 + 1):
            for kind, back in ((score, 0), (top, 1), (power, 1), (mix, 1)):
                for h in (2 * (pair - back), 2 * (pair - back) + 1):
                    if 0 <= h < HEADS:
                        steps.append(functools.partial(kind, h))
        return steps

    def leave_attention(slot):
        for n in range(0, D, 256):
            cols = slice(n, n + 256)
            xb[slot, :, cols] = (xs[:, cols].astype(F32) + dot(ms[...], value_map[:, cols])).astype(BF)

    def gate_steps():
        def step(n):
            cols = slice(n, n + 256)
            gate = dot(h2[...], vg[:, cols])
            up = dot(h2[...], vu[:, cols])
            hid[:, cols] = (jax.nn.silu(gate) * up).astype(BF)

        return [functools.partial(step, n) for n in range(0, FF, 256)]

    def down_steps(slot):
        def step(n):
            cols = slice(n, n + 256)
            fin[:, cols] = (xb[slot, :, cols].astype(F32) + dot(hid[...], vd[:, cols])).astype(BF)

        return [functools.partial(step, n) for n in range(0, D, 256)]

    def finish(c):
        interleave(norm_steps(hs, lambda rows: fin[rows, :], None))
        out[c] = dot(hs[...], vh[...]).astype(BF)

    interleave(attention_steps(enter(0)))
    middle(2)
    leave_attention(0)
    interleave(norm_steps(h2, lambda rows: xb[0, rows, :], 1))

    def chunk(c, _):
        slot = lax.rem(c, 2)
        gates = gate_steps()
        interleave(gates[:4])
        pl.when(c < CHUNKS - 3)(lambda: middle(c + 3))
        both = enter(c + 1)
        pl.when(c < CHUNKS - 2)(lambda: reduce(c + 2))
        interleave(attention_steps(both), gates[4:])
        leave_attention(1 - slot)
        interleave(down_steps(slot), norm_steps(h2, lambda rows: xb[1 - slot, rows, :], 1))
        finish(c)
        return 0

    lax.fori_loop(0, CHUNKS - 1, chunk, 0)
    interleave(gate_steps())
    interleave(down_steps((CHUNKS - 1) % 2))
    finish(CHUNKS - 1)

    def drain(c, _):
        copy_sum_a(c).wait_send()
        all_sum_b(c).wait_send()
        all_tiles(c).wait_send()
        return 0

    parts_left(CHUNKS - 1)
    lax.fori_loop(0, CHUNKS, drain, 0)


def body(spectra, w_embed, w_query, w_key, w_value, w_out, norm_gains, w_gate, w_up, w_down, w_head):
    vmem, dma = pltpu.VMEM, pltpu.SemaphoreType.DMA
    hbm = pl.BlockSpec(memory_space=pl.ANY)
    near = pl.BlockSpec(memory_space=pltpu.VMEM)
    result = pl.pallas_call(
        kernel,
        out_shape=jax.ShapeDtypeStruct((CHUNKS, ROWS, 2 * SLOTS), BF),
        in_specs=[hbm] * 8 + [near] + [hbm] * 4,
        out_specs=near,
        scratch_shapes=[
            vmem((2, 4, 2, 256, 384), BF),
            vmem((768, 512), BF),
            vmem((768, 512), BF),
            vmem((512, 512), BF),
            vmem((2 * SLOTS, D), BF),
            vmem((D, D), BF),
            vmem((D, D), BF),
            vmem((D, D), BF),
            vmem((D, D), BF),
            vmem((D, FF), BF),
            vmem((D, FF), BF),
            vmem((FF, D), BF),
            vmem((D, 2 * SLOTS), BF),
            vmem((CHUNKS, YN, XN, HALF, 128), BF),
            vmem((CHUNKS, XN, YN, HALF, 128), BF),
            vmem((CHUNKS, YN - 1, XN, HALF, 128), BF),
            vmem((CHUNKS, YN, HALF, 128), BF),
            vmem((CHUNKS, XN, HALF, 128), BF),
            vmem((CHUNKS, YN, HALF, 128), BF),
            vmem((CHUNKS, HALF, 128), BF),
            vmem((CHUNKS, YN - 1, HALF, 128), BF),
            vmem((CHUNKS, TM, 16, 128), BF),
            vmem((CHUNKS, TM, 16, 128), BF),
            vmem((ROWS, 128), F32),
            vmem((ROWS, 128), BF),
            vmem((ROWS, D), BF),
            vmem((ROWS, D), BF),
            vmem((ROWS, D), BF),
            vmem((ROWS, FF), BF),
            vmem((2, ROWS, D), BF),
            vmem((ROWS, D), BF),
            vmem((ROWS, D), BF),
            vmem((2 * SLOTS, D), BF),
            vmem((2 * SLOTS, D), BF),
            vmem((2 * SLOTS, D), BF),
            vmem((2 * SLOTS, D), BF),
            vmem((2 * SLOTS, D), BF),
            vmem((D, D), BF),
            dma((14,)),
            dma((5, CHUNKS)),
            dma((5, CHUNKS)),
            pltpu.SemaphoreType.REGULAR((2,)),
        ],
        compiler_params=pltpu.CompilerParams(collective_id=0, has_side_effects=True, vmem_limit_bytes=58 << 20),
        name="fused",
    )(
        spectra, jnp.asarray(delay_tables()), jnp.asarray(doppler_tables()),
        w_embed, w_query, w_key, w_value, w_out, norm_gains, w_gate, w_up, w_down, w_head,
    )
    return result.reshape(2, 16, TILE, 2 * SLOTS)


def solution(mesh):
    placed = (P(None, "tm", None, None, "freq"), P(), P(), P(), P(), P(), P(), P(), P(), P(), P())
    return jax.shard_map(
        body, mesh=mesh, in_specs=placed, out_specs=P(None, "tm", "freq", None), check_vma=False
    )
```
